32 devices in a mesh: dp: 16 (over z, x, core), seq: 2 (over y).
Axes of the slice: x: 2, y: 2, z: 4, core: 2. Of those that a mesh axis runs over, the one named last changes fastest.
Arguments:
- hidden_in: bfloat16 [16384, 2048], P(('dp', 'seq')), may hold values from -6 to 6
- norm_gain: float32 [2048], replicated, may hold values from 0.1 to 1.9
- w_qk: bfloat16 [2048, 3072], P(('dp', 'seq')), may hold values from -1 to 1
- w_v: bfloat16 [2048, 1024], P(('dp', 'seq')), may hold values from -0.125 to 0.125
- w_o: bfloat16 [2048, 2048], P(('dp', 'seq')), may hold values from -0.125 to 0.125
- prompt_pages: int32 [16], replicated, may hold values from 1 to 17, 128 in all
- last_fill: int32 [16], replicated, may hold values from 1 to 128
- page_slots: int32 [128], P('dp'), may hold values from 0 to 7, as said below
Outputs:
- attended: bfloat16 [16384, 2048], P(('dp', 'seq'))
- key_cache: bfloat16 [128, 128, 1024], P(('dp', 'seq'))
- value_cache: bfloat16 [128, 128, 1024], P(('dp', 'seq'))
The draws below stay inside these ranges and needn't reach their ends.
Inputs may be any that keep to these rules, and one draw needn't show every extreme that they name: `prompt_pages`: the prompts' pages lie end to end from position 0 and add up to 128. `page_slots`: each aligned run of 8 entries is a permutation of 0 to 7.
All inputs are finite; a program needn't handle non-finite values.
Results may differ from the reference program's by a relative error of at most 0.01.
The reference program's roundings to bfloat16 on the way (of `normed`, `queries`, `keys`, `values`, `weights` and `attn`) count: a program that leaves them out, or rounds other values in their place, can miss the bound.
Values may be sent and summed in bfloat16 or wider, within the bound.
A program may use at most 192 MiB of HBM per device.

```python
import math
import jax
import jax.numpy as jnp
import numpy as np
from jax import lax

D = 2048
HEADS = 16
KV_HEADS = 8
HEAD_DIM = 128
TOK_DEV = 512
PAGE = 128
REACH = 4
MAXPG = 17
TOKENS = 16384
NPAGES = 128
NREQ = 16
GROUP_PAGES = 8


def draw_w_qk(key, part):
    columns = (HEADS + KV_HEADS) * HEAD_DIM
    base = jax.random.truncated_normal(key, -4.0, 4.0, (D, columns), jnp.float32) / math.sqrt(D)
    return jnp.clip(base, -1.0, 1.0).astype(jnp.bfloat16)


def draw_page_slots(key, part):
    groups = NPAGES // GROUP_PAGES
    group_keys = jax.random.split(jax.random.fold_in(key, 3), groups)
    orders = jax.vmap(lambda single: jax.random.permutation(single, GROUP_PAGES))(group_keys)
    return orders.reshape(NPAGES).astype(jnp.int32)


def place_ends(drawn, rng, smallest, top_value):
    index_at = [jax.random.randint(jax.random.fold_in(rng, axis), (), 0, length) for axis, length in enumerate(drawn.shape)]
    longest = drawn.shape.index(max(drawn.shape))
    next_to = index_at[:longest] + [(index_at[longest] + 1) % drawn.shape[longest]] + index_at[longest + 1:]
    return drawn.at[tuple(index_at)].set(smallest).at[tuple(next_to)].set(top_value)


def level_of(key, dims, pieces, smallest, top_value):
    level = 1.0
    for dim, blocks in pieces:
        steps = jax.random.uniform(jax.random.fold_in(jax.random.fold_in(key, 6), dim), (blocks,), jnp.float32, smallest / len(pieces), top_value / len(pieces))
        level = level * jnp.repeat(jnp.exp(steps), dims[dim] // blocks).reshape((-1,) + (1,) * (len(dims) - 1 - dim))
    return level


def split_up(amount, total, limit, skew):
    portions = [(1 << 20) // math.isqrt(rank ** skew) + 1 for rank in range(2, amount + 1)]
    surplus, holding = total - limit - (amount - 1), [1] * (amount - 1)
    while surplus > 0:
        movable = [i for i in range(amount - 1) if holding[i] < limit]
        pool, left = sum([portions[i] for i in movable]), surplus
        for i in movable:
            addition = min(limit - holding[i], max(1, left * portions[i] // pool), surplus)
            holding[i] = holding[i] + addition
            surplus = surplus - addition
    return np.array([limit] + holding)


def ragged_sizes(own_key, number_of, total, reach, slope):
    if number_of == 2:
        one = jax.random.randint(own_key, (), max(1, total - reach), min(reach, total - 1) + 1)
        return jnp.stack([one, total - one])
    sizes = jnp.asarray(split_up(number_of, total, reach, slope), jnp.int32)
    couples = (number_of - 1) // 2
    source_of, sink = sizes[1:1 + 2 * couples:2], sizes[2:2 + 2 * couples:2]
    room = jnp.minimum(source_of - 1, reach - sink)
    passed = jax.random.randint(jax.random.fold_in(own_key, 1), (couples,), 0, 1 << 20) % (room + 1)
    sizes = sizes.at[1:1 + 2 * couples:2].set(source_of - passed).at[2:2 + 2 * couples:2].set(sink + passed)
    return sizes[jax.random.permutation(jax.random.fold_in(own_key, 2), number_of)]


def gaussian(stream_key, shape, spread, limit, shards=(), kind=jnp.bfloat16):
    entries = spread * jax.random.normal(stream_key, shape, jnp.float32)
    if shards:
        entries = entries * level_of(stream_key, shape, shards, -0.22, 0.18)
    return jnp.clip(entries, -limit, limit).astype(kind)


def setup_inputs(seed: int = 0) -> dict:
    key_list = jax.random.split(jax.random.key(seed), 9)
    return {
        "hidden_in": gaussian(key_list[0], (TOKENS, D), 1.0, 6.0, ((0, 32),)),
        "norm_gain": jnp.clip(1.0 + 0.18 * jax.random.normal(key_list[1], (D,), jnp.float32), 0.1, 1.9),
        "w_qk": draw_w_qk(jax.random.fold_in(key_list[8], 71), 0),
        "w_v": gaussian(key_list[3], (D, KV_HEADS * HEAD_DIM), D ** -0.5, 0.125, ((0, 32),)),
        "w_o": gaussian(key_list[4], (HEADS * HEAD_DIM, D), (HEADS * HEAD_DIM) ** -0.5, 0.125, ((0, 32),)),
        "prompt_pages": ragged_sizes(key_list[5], NREQ, NPAGES, MAXPG, 2).astype(jnp.int32),
        "last_fill": place_ends(jax.random.randint(key_list[6], (NREQ,), 1, PAGE + 1), jax.random.fold_in(key_list[6], 1), 1, PAGE).astype(jnp.int32),
        "page_slots": draw_page_slots(jax.random.fold_in(key_list[8], 71), 0),
    }


THETA = 1000000.0
EPS = 1e-05
NEG = -1e+30

def token_tables(prompt_pages, last_fill):
    ends = (jnp.cumsum(prompt_pages) * PAGE).astype(jnp.int32)
    starts = (ends - prompt_pages * PAGE).astype(jnp.int32)
    lengths = ((prompt_pages - 1) * PAGE + last_fill).astype(jnp.int32)
    return (starts, lengths)

def locate(token_ids, starts, lengths):
    inside = (token_ids[:, None] >= starts[None, :]).astype(jnp.int32)
    request = (lax.optimization_barrier(jnp.sum(inside, axis=1)) - 1).astype(jnp.int32)
    match = jnp.arange(starts.shape[0], dtype=jnp.int32)[None, :] == request[:, None]
    start = lax.optimization_barrier(jnp.sum(jnp.where(match, starts[None, :], 0), axis=1)).astype(jnp.int32)
    length = lax.optimization_barrier(jnp.sum(jnp.where(match, lengths[None, :], 0), axis=1)).astype(jnp.int32)
    position = (token_ids - start).astype(jnp.int32)
    valid = (position < length) & (token_ids >= 0)
    return (request, position, valid)

def pair_mask(query_ids, key_ids, starts, lengths):
    query_req, _, query_valid = locate(query_ids, starts, lengths)
    key_req, _, key_valid = locate(key_ids, starts, lengths)
    allowed = (query_req[:, None] == key_req[None, :]) & (key_ids[None, :] <= query_ids[:, None])
    return (allowed & query_valid[:, None] & key_valid[None, :], query_valid)

def rotate(heads, position):
    half = heads.shape[-1] // 2
    freq = jnp.power(THETA, -2.0 * jnp.arange(half, dtype=jnp.float32) / heads.shape[-1])
    angle = position.astype(jnp.float32)[:, None] * freq[None, :]
    cosine = jnp.concatenate([jnp.cos(angle), jnp.cos(angle)], axis=-1)[:, None, :]
    sine = jnp.concatenate([jnp.sin(angle), jnp.sin(angle)], axis=-1)[:, None, :]
    turned = jnp.concatenate([-heads[..., half:], heads[..., :half]], axis=-1)
    return heads * cosine + turned * sine

def normalize(hidden_in, norm_gain):
    values = hidden_in.astype(jnp.float32)
    scale = lax.rsqrt(lax.optimization_barrier(jnp.mean(values * values, axis=-1, keepdims=True)) + EPS)
    return (values * scale * norm_gain.astype(jnp.float32)[None, :]).astype(jnp.bfloat16)

def split_heads(projected, value_part, position):
    count = projected.shape[0]
    width = HEADS * HEAD_DIM
    queries = rotate(projected[:, :width].reshape(count, HEADS, HEAD_DIM), position)
    queries = queries.astype(jnp.bfloat16).reshape(count, width)
    keys = rotate(projected[:, width:].reshape(count, KV_HEADS, HEAD_DIM), position)
    keys = keys.astype(jnp.bfloat16).reshape(count, KV_HEADS * HEAD_DIM)
    return (queries, keys, value_part.astype(jnp.bfloat16))

def reference(hidden_in, norm_gain, w_qk, w_v, w_o, prompt_pages, last_fill, page_slots):
    starts, lengths = token_tables(prompt_pages, last_fill)
    token_ids = jnp.arange(TOKENS, dtype=jnp.int32)
    _, position, valid = locate(token_ids, starts, lengths)
    normed = normalize(hidden_in, norm_gain)
    projected = jnp.dot(normed, w_qk, preferred_element_type=jnp.float32)
    value_part = jnp.dot(normed, w_v, preferred_element_type=jnp.float32)
    queries, keys, values = split_heads(projected, value_part, position)
    span = REACH * TOK_DEV
    width = KV_HEADS * HEAD_DIM
    front = jnp.zeros((span, width), jnp.bfloat16)
    keys_padded = jnp.concatenate([front, keys], axis=0)
    values_padded = jnp.concatenate([front, values], axis=0)
    group = HEADS // KV_HEADS
    scale = 1.0 / math.sqrt(HEAD_DIM)

    def one_block(index):
        first = (index * TOK_DEV).astype(jnp.int32)
        query_ids = (first + jnp.arange(TOK_DEV, dtype=jnp.int32)).astype(jnp.int32)
        key_ids = (first - span + jnp.arange(span + TOK_DEV, dtype=jnp.int32)).astype(jnp.int32)
        mask, query_valid = pair_mask(query_ids, key_ids, starts, lengths)
        query_rows = lax.dynamic_slice_in_dim(queries, first, TOK_DEV).astype(jnp.float32)
        query_rows = query_rows.reshape(TOK_DEV, KV_HEADS, group, HEAD_DIM)
        key_rows = lax.dynamic_slice_in_dim(keys_padded, first, span + TOK_DEV).astype(jnp.float32)
        key_rows = key_rows.reshape(span + TOK_DEV, KV_HEADS, HEAD_DIM)
        value_rows = lax.dynamic_slice_in_dim(values_padded, first, span + TOK_DEV).astype(jnp.float32)
        value_rows = value_rows.reshape(span + TOK_DEV, KV_HEADS, HEAD_DIM)
        scores = jnp.einsum('qkgd,skd->kgqs', query_rows, key_rows) * scale
        scores = jnp.where(mask[None, None], scores, NEG)
        top = lax.optimization_barrier(jnp.max(scores, axis=-1))
        expo = jnp.where(mask[None, None], jnp.exp(scores - top[..., None]), 0.0)
        total = lax.optimization_barrier(jnp.sum(expo, axis=-1))
        weights = lax.optimization_barrier(expo.astype(jnp.bfloat16)).astype(jnp.float32)
        numer = jnp.einsum('kgqs,skd->kgqd', weights, value_rows)
        safe = jnp.where(query_valid[None, None, :], total, 1.0)
        result = jnp.where(query_valid[None, None, :, None], numer / safe[..., None], 0.0)
        return result.transpose(2, 0, 1, 3).reshape(TOK_DEV, HEADS * HEAD_DIM).astype(jnp.bfloat16)
    attn = lax.map(one_block, jnp.arange(TOKENS // TOK_DEV, dtype=jnp.int32))
    attn = attn.reshape(TOKENS, HEADS * HEAD_DIM)
    attended = jnp.dot(attn, w_o, preferred_element_type=jnp.float32).astype(jnp.bfloat16)
    kept_keys = jnp.where(valid[:, None], keys, jnp.zeros_like(keys)).reshape(NPAGES, PAGE, width)
    kept_values = jnp.where(valid[:, None], values, jnp.zeros_like(values)).reshape(NPAGES, PAGE, width)
    page_ids = jnp.arange(NPAGES, dtype=jnp.int32)
    target = (page_ids // GROUP_PAGES * GROUP_PAGES + page_slots).astype(jnp.int32)
    key_cache = jnp.zeros((NPAGES, PAGE, width), jnp.bfloat16).at[target].set(kept_keys)
    value_cache = jnp.zeros((NPAGES, PAGE, width), jnp.bfloat16).at[target].set(kept_values)
    return (attended, key_cache, value_cache)
```

```python
import functools
import math

import jax
import jax.numpy as jnp
from jax import lax
from jax.experimental import pallas as pl
from jax.experimental.pallas import tpu as pltpu
from jax.sharding import Mesh, PartitionSpec as P

HEADS = 16
KV_HEADS = 8
HEAD_DIM = 128
PAGE = 128
GROUP = 4
CHUNK = 4
THETA = 1000000.0
EPS = 1e-05
NEG = -1e30
VMEM = 56 * 1024 * 1024

Q_COLS = HEADS * HEAD_DIM // GROUP
KV_COLS = KV_HEADS * HEAD_DIM // GROUP
KV_PER = KV_HEADS // GROUP
SHARE = HEADS // KV_HEADS


def normalize(hidden_in, norm_gain):
    values = hidden_in.astype(jnp.float32)
    scale = lax.rsqrt(jnp.mean(values * values, axis=-1, keepdims=True) + EPS)
    return (values * scale * norm_gain[None, :]).astype(jnp.bfloat16)


def page_tables(first_page, pages, prompt_pages, last_fill):
    ends = jnp.cumsum(prompt_pages)
    starts = ends - prompt_pages
    ids = first_page + jnp.arange(pages, dtype=jnp.int32)
    mine = (ids[:, None] >= starts[None, :]) & (ids[:, None] < ends[None, :])
    start = jnp.sum(jnp.where(mine, starts[None, :], 0), axis=1)
    end = jnp.sum(jnp.where(mine, ends[None, :], 0), axis=1)
    fill = jnp.sum(jnp.where(mine, last_fill[None, :], 0), axis=1)
    back = ids - start
    live = jnp.where(ids == end - 1, fill, PAGE)
    return back.astype(jnp.int32), live.astype(jnp.int32)


def rope_tables(back, pages):
    half = HEAD_DIM // 2
    position = (back[:, None] * PAGE + jnp.arange(PAGE, dtype=jnp.int32)[None, :]).reshape(pages * PAGE)
    freq = jnp.power(THETA, -2.0 * jnp.arange(half, dtype=jnp.float32) / HEAD_DIM)
    angle = position.astype(jnp.float32)[:, None] * freq[None, :]
    cosine, sine = jnp.cos(angle), jnp.sin(angle)
    return jnp.concatenate([cosine, cosine], axis=-1), jnp.concatenate([-sine, sine], axis=-1)


def project_body(rotated, spot, x0, x1, x2, x3, w, cosine, sine, *rest):
    outs, held = rest[:-1], rest[-1]
    step = pl.program_id(0)
    for index, x in enumerate((x0, x1, x2, x3)):

        @pl.when(step == index)
        def _(x=x):
            held[...] = x[...]

    tile = 256

    def rows(r, carry):
        at = pl.ds(pl.multiple_of(r * tile, tile), tile)
        product = jnp.dot(held[at, :], w[...], preferred_element_type=jnp.float32)
        c, s = cosine[at, :], sine[at, :]
        column = 0
        for out in outs:
            for head in range(out.shape[1] // HEAD_DIM):
                part = product[:, column : column + HEAD_DIM]
                if column < rotated:
                    part = part * c + pltpu.roll(part, HEAD_DIM // 2, 1) * s
                out[at, head * HEAD_DIM : (head + 1) * HEAD_DIM] = part.astype(jnp.bfloat16)
                column += HEAD_DIM
        return carry

    lax.fori_loop(0, held.shape[0] // tile, rows, 0)


def project(spot, blocks, weights, half, cosine, sine, widths, rotated):
    rows, depth = blocks[0].shape
    columns = sum(widths)
    whole = pl.BlockSpec((rows, depth), lambda s, spot: (0, 0))
    table = pl.BlockSpec((rows, HEAD_DIM), lambda s, spot: (spot[s], 0))
    return pl.pallas_call(
        functools.partial(project_body, rotated),
        grid_spec=pltpu.PrefetchScalarGridSpec(
            num_scalar_prefetch=1,
            grid=(GROUP,),
            in_specs=[whole] * 4
            + [pl.BlockSpec((depth, columns), lambda s, spot: (0, half)), table, table],
            out_specs=[pl.BlockSpec((rows, width), lambda s, spot: (spot[s], 0)) for width in widths],
            scratch_shapes=[pltpu.VMEM((rows, depth), jnp.bfloat16)],
        ),
        out_shape=[jax.ShapeDtypeStruct((GROUP * rows, width), jnp.bfloat16) for width in widths],
        compiler_params=pltpu.CompilerParams(vmem_limit_bytes=VMEM),
        cost_estimate=pl.CostEstimate(
            flops=2 * GROUP * rows * depth * columns, bytes_accessed=GROUP * rows * (depth + columns) * 2, transcendentals=0
        ),
    )(spot, *blocks, weights, cosine, sine)


def attend_body(back, live, q, k_own, v_own, k_prev, v_prev, out, k_all, v_all):
    rows = q.shape[0]
    pages = rows // PAGE
    pad = CHUNK * PAGE
    wide = CHUNK * PAGE
    for buffer, prev, own in ((k_all, k_prev, k_own), (v_all, v_prev, v_own)):
        buffer[0:pad, :] = jnp.zeros((pad, KV_COLS), jnp.bfloat16)
        buffer[pad : pad + rows, :] = prev[...]
        buffer[pad + rows :, :] = own[...]
    factor = math.log2(math.e) / math.sqrt(HEAD_DIM)
    height = SHARE * PAGE
    row = lax.broadcasted_iota(jnp.int32, (height, wide), 0) % PAGE
    causal = lax.broadcasted_iota(jnp.int32, (height, wide), 1) - (wide - PAGE) <= row
    key_at = lax.broadcasted_iota(jnp.int32, (1, wide), 1)
    row_in = lax.broadcasted_iota(jnp.int32, (height, 1), 0) % PAGE

    def page_step(page, carry):
        reach = back[page]
        at = pl.ds(pl.multiple_of(page * PAGE, PAGE), PAGE)
        queries = [
            jnp.concatenate(
                [q[at, (h * SHARE + i) * HEAD_DIM : (h * SHARE + i + 1) * HEAD_DIM] for i in range(SHARE)], axis=0
            )
            for h in range(KV_PER)
        ]

        def chunk(index, state, diagonal):
            first = page + CHUNK + pages - (CHUNK - 1) - CHUNK * index
            where = pl.ds(pl.multiple_of(first * PAGE, PAGE), wide)
            low = (CHUNK - 1 + CHUNK * index - reach) * PAGE
            bias = jnp.where(key_at >= low, 0.0, NEG)
            fresh = []
            for h in range(KV_PER):
                keys = k_all[where, h * HEAD_DIM : (h + 1) * HEAD_DIM]
                values = v_all[where, h * HEAD_DIM : (h + 1) * HEAD_DIM]
                scores = lax.dot_general(
                    queries[h], keys, (((1,), (1,)), ((), ())), preferred_element_type=jnp.float32
                ) + bias
                if diagonal:
                    scores = jnp.where(causal, scores, NEG)
                best = jnp.max(scores, axis=1, keepdims=True)
                if not diagonal:
                    top, total, numer = state[h]
                    best = jnp.maximum(top, best)
                expo = jnp.exp2(scores * factor - best * factor)
                part = expo[:, 0:PAGE]
                for piece in range(1, CHUNK):
                    part = part + expo[:, piece * PAGE : (piece + 1) * PAGE]
                product = jnp.dot(expo.astype(jnp.bfloat16), values, preferred_element_type=jnp.float32)
                if not diagonal:
                    shrink = jnp.exp2(top * factor - best * factor)
                    part = total * shrink + part
                    product = numer * shrink + product
                fresh.append((best, part, product))
            return tuple(fresh)

        state = chunk(0, None, True)
        state = lax.fori_loop(1, reach // CHUNK + 1, lambda i, s: chunk(i, s, False), state)
        alive = row_in < live[page]
        for h in range(KV_PER):
            _, part, numer = state[h]
            total = jnp.sum(part, axis=1, keepdims=True)
            result = jnp.where(alive, numer / total, 0.0).astype(jnp.bfloat16)
            for i in range(SHARE):
                head = h * SHARE + i
                out[at, head * HEAD_DIM : (head + 1) * HEAD_DIM] = result[i * PAGE : (i + 1) * PAGE]
        return carry

    lax.fori_loop(0, pages, page_step, 0)


def attend(back, live, q, k_own, v_own, k_prev, v_prev):
    rows = q.shape[0]
    smem = pl.BlockSpec(memory_space=pltpu.SMEM)
    vmem = pl.BlockSpec(memory_space=pltpu.VMEM)
    span = 2 * rows + CHUNK * PAGE
    return pl.pallas_call(
        attend_body,
        in_specs=[smem, smem] + [vmem] * 5,
        out_specs=vmem,
        out_shape=jax.ShapeDtypeStruct(q.shape, jnp.bfloat16),
        scratch_shapes=[pltpu.VMEM((span, KV_COLS), jnp.bfloat16), pltpu.VMEM((span, KV_COLS), jnp.bfloat16)],
        compiler_params=pltpu.CompilerParams(vmem_limit_bytes=VMEM),
        cost_estimate=pl.CostEstimate(flops=12 * 10**9, bytes_accessed=8 * 2**20, transcendentals=10**7),
    )(back, live, q, k_own, v_own, k_prev, v_prev)


def pages_body(source, live, k, v, k_out, v_out):
    row = lax.broadcasted_iota(jnp.int32, (PAGE, 1), 0)

    def one(slot, carry):
        page = source[slot]
        at = pl.ds(pl.multiple_of(page * PAGE, PAGE), PAGE)
        keep = row < live[page]
        k_out[slot] = jnp.where(keep, k[at, :].astype(jnp.float32), 0.0).astype(jnp.bfloat16)
        v_out[slot] = jnp.where(keep, v[at, :].astype(jnp.float32), 0.0).astype(jnp.bfloat16)
        return carry

    lax.fori_loop(0, k_out.shape[0], one, 0)


def order_pages(source, live, k, v):
    smem = pl.BlockSpec(memory_space=pltpu.SMEM)
    vmem = pl.BlockSpec(memory_space=pltpu.VMEM)
    shape = jax.ShapeDtypeStruct((k.shape[0] // PAGE, PAGE, k.shape[1]), jnp.bfloat16)
    return pl.pallas_call(
        pages_body,
        in_specs=[smem, smem, vmem, vmem],
        out_specs=[vmem, vmem],
        out_shape=[shape, shape],
        compiler_params=pltpu.CompilerParams(vmem_limit_bytes=VMEM),
        cost_estimate=pl.CostEstimate(flops=10**6, bytes_accessed=4 * 2**20, transcendentals=0),
    )(source, live, k, v)


def output_body(a, w, out):
    depth = a.shape[2]
    total = jnp.dot(a[0], w[0:depth, :], preferred_element_type=jnp.float32)
    for index in range(1, a.shape[0]):
        total += jnp.dot(a[index], w[index * depth : (index + 1) * depth, :], preferred_element_type=jnp.float32)
    out[...] = total.astype(jnp.bfloat16)


def output(a, w):
    parts, rows, depth = a.shape
    columns, tile = w.shape[1], 256
    return pl.pallas_call(
        output_body,
        grid=(columns // tile,),
        in_specs=[
            pl.BlockSpec((parts, rows, depth), lambda n: (0, 0, 0)),
            pl.BlockSpec((parts * depth, tile), lambda n: (0, n)),
        ],
        out_specs=pl.BlockSpec((rows, tile), lambda n: (0, n)),
        out_shape=jax.ShapeDtypeStruct((rows, columns), jnp.bfloat16),
        compiler_params=pltpu.CompilerParams(vmem_limit_bytes=VMEM),
        cost_estimate=pl.CostEstimate(
            flops=2 * parts * rows * depth * columns, bytes_accessed=12 * 2**20, transcendentals=0
        ),
    )(a, w)


def shards(hidden_in, norm_gain, w_qk, w_v, w_o, prompt_pages, last_fill, page_slots):
    rows = hidden_in.shape[0]
    inside = ("c", "y")
    place = lax.axis_index("c") * 2 + lax.axis_index("y")
    pages = GROUP * rows // PAGE
    swap = [(0, 1), (1, 0)]

    width = HEADS * HEAD_DIM
    kv_width = KV_HEADS * HEAD_DIM
    depth = w_qk.shape[0]
    split = jnp.concatenate(
        [
            w_qk[:, width:].reshape(depth, GROUP, KV_COLS),
            w_v.reshape(depth, GROUP, KV_COLS),
            w_qk[:, :width].reshape(depth, GROUP, Q_COLS),
        ],
        axis=2,
    ).transpose(1, 0, 2)
    mine = lax.all_to_all(split, inside, split_axis=0, concat_axis=0, tiled=True)
    weights = lax.all_gather(mine.reshape(GROUP * depth, 2 * Q_COLS), "g", axis=0, tiled=True)

    normed = normalize(hidden_in, norm_gain)
    across = lax.ppermute(normed, "y", swap)
    core = lax.ppermute(normed, "c", swap)
    both = lax.ppermute(across, "c", swap)
    spot = jnp.arange(GROUP, dtype=jnp.int32) ^ place

    back, live = page_tables(lax.axis_index("g") * pages, pages, prompt_pages, last_fill)
    cosine, sine = rope_tables(back, pages)

    blocks = (normed, across, core, both)
    keys, values = project(spot, blocks, weights, 0, cosine, sine, (KV_COLS, KV_COLS), KV_COLS)
    groups = lax.axis_size("g")
    onward = [(i, i + 1) for i in range(groups - 1)]
    k_prev = lax.ppermute(keys, "g", onward)
    v_prev = lax.ppermute(values, "g", onward)
    (queries,) = project(spot, blocks, weights, 1, cosine, sine, (Q_COLS,), Q_COLS)

    slots = lax.all_gather(page_slots, "c", axis=0, tiled=False)
    order = jnp.arange(slots.shape[1], dtype=jnp.int32)
    hit = slots[:, None, :] == order[None, :, None]
    source = jnp.sum(jnp.where(hit, order[None, None, :], 0), axis=2)
    source = (source + jnp.arange(2, dtype=jnp.int32)[:, None] * slots.shape[1]).reshape(pages)
    k_pages, v_pages = order_pages(source.astype(jnp.int32), live, keys, values)
    key_cache = lax.all_to_all(k_pages, inside, split_axis=0, concat_axis=2, tiled=True)
    value_cache = lax.all_to_all(v_pages, inside, split_axis=0, concat_axis=2, tiled=True)

    w_out = lax.all_gather(w_o, ("g", "c", "y"), axis=0, tiled=True)
    attn = attend(back, live, queries, keys, values, k_prev, v_prev)
    own = lax.all_to_all(attn.reshape(GROUP, rows, Q_COLS), inside, split_axis=0, concat_axis=0, tiled=True)
    return (output(own, w_out), key_cache, value_cache)


def solution(mesh):
    fine = Mesh(mesh.devices.reshape(-1, 2, 2), ("g", "c", "y"))
    tokens = ("g", "c", "y")
    in_specs = (
        P(tokens, None),
        P(),
        P(tokens, None),
        P(tokens, None),
        P(tokens, None),
        P(),
        P(),
        P(("g", "c")),
    )
    out_specs = (P(tokens, None), P(tokens, None, None), P(tokens, None, None))
    return jax.shard_map(shards, mesh=fine, in_specs=in_specs, out_specs=out_specs, check_vma=False)
```

```python
import functools
import math

import jax
import jax.numpy as jnp
from jax import lax
from jax.experimental import pallas as pl
from jax.experimental.pallas import tpu as pltpu
from jax.sharding import Mesh, PartitionSpec as P

HEADS = 16
KV_HEADS = 8
HEAD_DIM = 128
PAGE = 128
GROUP = 4
CHUNK = 4
THETA = 1000000.0
EPS = 1e-05
NEG = -1e30
VMEM = 56 * 1024 * 1024

Q_COLS = HEADS * HEAD_DIM // GROUP
KV_COLS = KV_HEADS * HEAD_DIM // GROUP
KV_PER = KV_HEADS // GROUP
SHARE = HEADS // KV_HEADS


def normalize(hidden_in, norm_gain):
    values = hidden_in.astype(jnp.float32)
    scale = lax.rsqrt(jnp.mean(values * values, axis=-1, keepdims=True) + EPS)
    return (values * scale * norm_gain[None, :]).astype(jnp.bfloat16)


def page_tables(first_page, pages, prompt_pages, last_fill):
    ends = jnp.cumsum(prompt_pages)
    starts = ends - prompt_pages
    ids = first_page + jnp.arange(pages, dtype=jnp.int32)
    mine = (ids[:, None] >= starts[None, :]) & (ids[:, None] < ends[None, :])
    start = jnp.sum(jnp.where(mine, starts[None, :], 0), axis=1)
    end = jnp.sum(jnp.where(mine, ends[None, :], 0), axis=1)
    fill = jnp.sum(jnp.where(mine, last_fill[None, :], 0), axis=1)
    back = ids - start
    live = jnp.where(ids == end - 1, fill, PAGE)
    return back.astype(jnp.int32), live.astype(jnp.int32)


def rope_tables(back, pages):
    half = HEAD_DIM // 2
    position = (back[:, None] * PAGE + jnp.arange(PAGE, dtype=jnp.int32)[None, :]).reshape(pages * PAGE)
    freq = jnp.power(THETA, -2.0 * jnp.arange(half, dtype=jnp.float32) / HEAD_DIM)
    angle = position.astype(jnp.float32)[:, None] * freq[None, :]
    cosine, sine = jnp.cos(angle), jnp.sin(angle)
    return jnp.concatenate([cosine, cosine], axis=-1), jnp.concatenate([-sine, sine], axis=-1)


def project_body(rotated, spot, x0, x1, x2, x3, w, cosine, sine, *rest):
    outs, held = rest[:-1], rest[-1]
    step = pl.program_id(0)
    for index, x in enumerate((x0, x1, x2, x3)):

        @pl.when(step == index)
        def _(x=x):
            held[...] = x[...]

    tile = 512

    def rows(r, carry):
        at = pl.ds(pl.multiple_of(r * tile, tile), tile)
        product = jnp.dot(held[at, :], w[...], preferred_element_type=jnp.float32)
        c, s = cosine[at, :], sine[at, :]
        column = 0
        for out in outs:
            for head in range(out.shape[1] // HEAD_DIM):
                part = product[:, column : column + HEAD_DIM]
                if column < rotated:
                    part = part * c + pltpu.roll(part, HEAD_DIM // 2, 1) * s
                out[at, head * HEAD_DIM : (head + 1) * HEAD_DIM] = part.astype(jnp.bfloat16)
                column += HEAD_DIM
        return carry

    lax.fori_loop(0, held.shape[0] // tile, rows, 0)


def project(spot, blocks, weights, half, cosine, sine, widths, rotated):
    rows, depth = blocks[0].shape
    columns = sum(widths)
    whole = pl.BlockSpec((rows, depth), lambda s, spot: (0, 0))
    table = pl.BlockSpec((rows, HEAD_DIM), lambda s, spot: (spot[s], 0))
    return pl.pallas_call(
        functools.partial(project_body, rotated),
        grid_spec=pltpu.PrefetchScalarGridSpec(
            num_scalar_prefetch=1,
            grid=(GROUP,),
            in_specs=[whole] * 4
            + [pl.BlockSpec((depth, columns), lambda s, spot: (0, half)), table, table],
            out_specs=[pl.BlockSpec((rows, width), lambda s, spot: (spot[s], 0)) for width in widths],
            scratch_shapes=[pltpu.VMEM((rows, depth), jnp.bfloat16)],
        ),
        out_shape=[jax.ShapeDtypeStruct((GROUP * rows, width), jnp.bfloat16) for width in widths],
        compiler_params=pltpu.CompilerParams(vmem_limit_bytes=VMEM),
        cost_estimate=pl.CostEstimate(
            flops=2 * GROUP * rows * depth * columns, bytes_accessed=GROUP * rows * (depth + columns) * 2, transcendentals=0
        ),
    )(spot, *blocks, weights, cosine, sine)


def scan_chunk(queries, k, v, where, low, state, causal):
    wide = CHUNK * PAGE
    factor = math.log2(math.e) / math.sqrt(HEAD_DIM)
    bias = jnp.where(lax.broadcasted_iota(jnp.int32, (1, wide), 1) >= low, 0.0, NEG)
    fresh = []
    for h in range(KV_PER):
        keys = k[where, h * HEAD_DIM : (h + 1) * HEAD_DIM]
        values = v[where, h * HEAD_DIM : (h + 1) * HEAD_DIM]
        scores = lax.dot_general(
            queries[h], keys, (((1,), (1,)), ((), ())), preferred_element_type=jnp.float32
        ) + bias
        if causal is not None:
            scores = jnp.where(causal, scores, NEG)
        best = jnp.max(scores, axis=1, keepdims=True)
        if state is not None:
            top, total, numer = state[h]
            best = jnp.maximum(top, best)
        expo = jnp.exp2(scores * factor - best * factor)
        part = expo[:, 0:PAGE]
        for piece in range(1, CHUNK):
            part = part + expo[:, piece * PAGE : (piece + 1) * PAGE]
        product = jnp.dot(expo.astype(jnp.bfloat16), values, preferred_element_type=jnp.float32)
        if state is not None:
            shrink = jnp.exp2(top * factor - best * factor)
            part = total * shrink + part
            product = numer * shrink + product
        fresh.append((best, part, product))
    return tuple(fresh)


def query_tiles(q, page):
    at = pl.ds(pl.multiple_of(page * PAGE, PAGE), PAGE)
    return [
        jnp.concatenate(
            [q[at, (h * SHARE + i) * HEAD_DIM : (h * SHARE + i + 1) * HEAD_DIM] for i in range(SHARE)], axis=0
        )
        for h in range(KV_PER)
    ]


def page_at(index, pages):
    per_block = pages // GROUP
    per_half = per_block // 2
    half, rest = lax.div(index, pages // 2), lax.rem(index, pages // 2)
    return lax.div(rest, per_half) * per_block + half * per_half + lax.rem(rest, per_half)


def near_body(back, q, k_own, v_own, stats, sums, k_all, v_all):
    rows = q.shape[0]
    pages = rows // PAGE
    pad = CHUNK * PAGE
    wide = CHUNK * PAGE
    for buffer, own in ((k_all, k_own), (v_all, v_own)):
        buffer[0:pad, :] = jnp.zeros((pad, KV_COLS), jnp.bfloat16)
        buffer[pad:, :] = own[...]
    height = SHARE * PAGE
    row = lax.broadcasted_iota(jnp.int32, (height, wide), 0) % PAGE
    causal = lax.broadcasted_iota(jnp.int32, (height, wide), 1) - (wide - PAGE) <= row
    lower = lax.broadcasted_iota(jnp.int32, (height, HEAD_DIM), 1) < HEAD_DIM // 2

    def page_step(index, carry):
        page = page_at(index, pages)
        reach = jnp.minimum(back[page], page)
        queries = query_tiles(q, page)

        def chunk(i, state, mask):
            first = page + 1 - CHUNK * i
            where = pl.ds(pl.multiple_of(first * PAGE, PAGE), wide)
            low = (CHUNK - 1 + CHUNK * i - reach) * PAGE
            return scan_chunk(queries, k_all, v_all, where, low, state, mask)

        state = chunk(0, None, causal)
        state = lax.fori_loop(1, lax.div(reach, CHUNK) + 1, lambda i, s: chunk(i, s, None), state)
        for h in range(KV_PER):
            best, part, numer = state[h]
            total = jnp.sum(part, axis=1, keepdims=True)
            stats[index, h] = jnp.where(lower, best, total)
            sums[index, h] = numer
        return carry

    lax.fori_loop(0, pages, page_step, 0)


def attend_near(back, q, k_own, v_own):
    rows = q.shape[0]
    smem = pl.BlockSpec(memory_space=pltpu.SMEM)
    vmem = pl.BlockSpec(memory_space=pltpu.VMEM)
    span = rows + CHUNK * PAGE
    state = jax.ShapeDtypeStruct((rows // PAGE, KV_PER, SHARE * PAGE, HEAD_DIM), jnp.float32)
    return pl.pallas_call(
        near_body,
        in_specs=[smem] + [vmem] * 3,
        out_specs=[vmem, vmem],
        out_shape=[state, state],
        scratch_shapes=[pltpu.VMEM((span, KV_COLS), jnp.bfloat16), pltpu.VMEM((span, KV_COLS), jnp.bfloat16)],
        compiler_params=pltpu.CompilerParams(vmem_limit_bytes=VMEM),
        cost_estimate=pl.CostEstimate(flops=12 * 10**9, bytes_accessed=12 * 2**20, transcendentals=10**7),
    )(back, q, k_own, v_own)


def far_body(half, back, live, q, k_prev, v_prev, stats, sums, out):
    rows = q.shape[0]
    pages = rows // PAGE
    wide = CHUNK * PAGE
    height = SHARE * PAGE
    row_in = lax.broadcasted_iota(jnp.int32, (height, 1), 0) % PAGE
    lane = lax.broadcasted_iota(jnp.int32, (height, HEAD_DIM), 1)

    def page_step(index, carry):
        page = page_at(index + half * (pages // 2), pages)
        count = jnp.maximum(back[page] - page, 0)
        queries = query_tiles(q, page)
        state = []
        for h in range(KV_PER):
            pair = stats[index, h]
            best = pair[:, 0:1]
            total = jnp.where(lane == HEAD_DIM // 2, pair, 0.0)
            state.append((best, total, sums[index, h]))

        def chunk(i, state):
            first = pages - CHUNK - CHUNK * i
            where = pl.ds(pl.multiple_of(first * PAGE, PAGE), wide)
            low = (CHUNK + CHUNK * i - count) * PAGE
            return scan_chunk(queries, k_prev, v_prev, where, low, state, None)

        state = lax.fori_loop(0, lax.div(count + CHUNK - 1, CHUNK), chunk, tuple(state))
        alive = row_in < live[page]
        at = pl.ds(pl.multiple_of(index * PAGE, PAGE), PAGE)
        for h in range(KV_PER):
            _, part, numer = state[h]
            total = jnp.sum(part, axis=1, keepdims=True)
            result = jnp.where(alive, numer / total, 0.0).astype(jnp.bfloat16)
            for i in range(SHARE):
                head = h * SHARE + i
                out[at, head * HEAD_DIM : (head + 1) * HEAD_DIM] = result[i * PAGE : (i + 1) * PAGE]
        return carry

    lax.fori_loop(0, pages // 2, page_step, 0)


def attend_far(half, back, live, q, k_prev, v_prev, stats, sums):
    rows = q.shape[0]
    pages = rows // PAGE
    smem = pl.BlockSpec(memory_space=pltpu.SMEM)

    def whole(shape):
        return pl.BlockSpec(shape, lambda n: (0, 0))

    state = pl.BlockSpec((pages // 2,) + stats.shape[1:], lambda n: (half, 0, 0, 0))
    return pl.pallas_call(
        functools.partial(far_body, half),
        grid=(1,),
        in_specs=[smem, smem, whole(q.shape), whole(k_prev.shape), whole(v_prev.shape), state, state],
        out_specs=whole((rows // 2, q.shape[1])),
        out_shape=jax.ShapeDtypeStruct((rows // 2, q.shape[1]), jnp.bfloat16),
        compiler_params=pltpu.CompilerParams(vmem_limit_bytes=VMEM),
        cost_estimate=pl.CostEstimate(flops=4 * 10**9, bytes_accessed=10 * 2**20, transcendentals=4 * 10**6),
    )(back, live, q, k_prev, v_prev, stats, sums)


def pages_body(source, live, k, v, k_out, v_out):
    row = lax.broadcasted_iota(jnp.int32, (PAGE, 1), 0)

    def one(slot, carry):
        page = source[slot]
        at = pl.ds(pl.multiple_of(page * PAGE, PAGE), PAGE)
        keep = row < live[page]
        k_out[slot] = jnp.where(keep, k[at, :].astype(jnp.float32), 0.0).astype(jnp.bfloat16)
        v_out[slot] = jnp.where(keep, v[at, :].astype(jnp.float32), 0.0).astype(jnp.bfloat16)
        return carry

    lax.fori_loop(0, k_out.shape[0], one, 0)


def order_pages(source, live, k, v):
    smem = pl.BlockSpec(memory_space=pltpu.SMEM)
    vmem = pl.BlockSpec(memory_space=pltpu.VMEM)
    shape = jax.ShapeDtypeStruct((k.shape[0] // PAGE, PAGE, k.shape[1]), jnp.bfloat16)
    return pl.pallas_call(
        pages_body,
        in_specs=[smem, smem, vmem, vmem],
        out_specs=[vmem, vmem],
        out_shape=[shape, shape],
        compiler_params=pltpu.CompilerParams(vmem_limit_bytes=VMEM),
        cost_estimate=pl.CostEstimate(flops=10**6, bytes_accessed=4 * 2**20, transcendentals=0),
    )(source, live, k, v)


def output_body(*refs):
    w, out = refs[-2:]
    row = 0
    for a in refs[:-2]:
        rows, depth = a.shape[1:]
        total = jnp.dot(a[0], w[0:depth, :], preferred_element_type=jnp.float32)
        for index in range(1, a.shape[0]):
            total += jnp.dot(a[index], w[index * depth : (index + 1) * depth, :], preferred_element_type=jnp.float32)
        out[row : row + rows, :] = total.astype(jnp.bfloat16)
        row += rows


def output(halves, w):
    parts, rows, depth = halves[0].shape
    columns, tile = w.shape[1], 512
    height = rows * len(halves)
    return pl.pallas_call(
        output_body,
        grid=(columns // tile,),
        in_specs=[pl.BlockSpec((parts, rows, depth), lambda n: (0, 0, 0)) for _ in halves]
        + [pl.BlockSpec((parts * depth, tile), lambda n: (0, n))],
        out_specs=pl.BlockSpec((height, tile), lambda n: (0, n)),
        out_shape=jax.ShapeDtypeStruct((height, columns), jnp.bfloat16),
        compiler_params=pltpu.CompilerParams(vmem_limit_bytes=VMEM),
        cost_estimate=pl.CostEstimate(
            flops=2 * parts * height * depth * columns, bytes_accessed=12 * 2**20, transcendentals=0
        ),
    )(*halves, w)


def shards(hidden_in, norm_gain, w_qk, w_v, w_o, prompt_pages, last_fill, page_slots):
    rows = hidden_in.shape[0]
    inside = ("c", "y")
    place = lax.axis_index("c") * 2 + lax.axis_index("y")
    pages = GROUP * rows // PAGE
    swap = [(0, 1), (1, 0)]

    width = HEADS * HEAD_DIM
    kv_width = KV_HEADS * HEAD_DIM
    depth = w_qk.shape[0]
    split = jnp.concatenate(
        [
            w_qk[:, width:].reshape(depth, GROUP, KV_COLS),
            w_v.reshape(depth, GROUP, KV_COLS),
            w_qk[:, :width].reshape(depth, GROUP, Q_COLS),
        ],
        axis=2,
    ).transpose(1, 0, 2)
    mine = lax.all_to_all(split, inside, split_axis=0, concat_axis=0, tiled=True)
    weights = lax.all_gather(mine.reshape(GROUP * depth, 2 * Q_COLS), "g", axis=0, tiled=True)

    normed = normalize(hidden_in, norm_gain)
    across = lax.ppermute(normed, "y", swap)
    core = lax.ppermute(normed, "c", swap)
    both = lax.ppermute(across, "c", swap)
    spot = jnp.arange(GROUP, dtype=jnp.int32) ^ place

    back, live = page_tables(lax.axis_index("g") * pages, pages, prompt_pages, last_fill)
    cosine, sine = rope_tables(back, pages)

    blocks = (normed, across, core, both)
    keys, values = project(spot, blocks, weights, 0, cosine, sine, (KV_COLS, KV_COLS), KV_COLS)
    groups = lax.axis_size("g")
    onward = [(i, i + 1) for i in range(groups - 1)]
    k_prev = lax.ppermute(keys, "g", onward)
    v_prev = lax.ppermute(values, "g", onward)
    (queries,) = project(spot, blocks, weights, 1, cosine, sine, (Q_COLS,), Q_COLS)

    slots = lax.all_gather(page_slots, "c", axis=0, tiled=False)
    order = jnp.arange(slots.shape[1], dtype=jnp.int32)
    hit = slots[:, None, :] == order[None, :, None]
    source = jnp.sum(jnp.where(hit, order[None, None, :], 0), axis=2)
    source = (source + jnp.arange(2, dtype=jnp.int32)[:, None] * slots.shape[1]).reshape(pages)
    k_pages, v_pages = order_pages(source.astype(jnp.int32), live, keys, values)
    same = lax.all_gather(w_o, ("g", "y"), axis=0, tiled=True)
    early, k_pages, v_pages = lax.optimization_barrier((queries, k_pages, v_pages))
    key_cache = lax.all_to_all(k_pages, inside, split_axis=0, concat_axis=2, tiled=True)
    value_cache = lax.all_to_all(v_pages, inside, split_axis=0, concat_axis=2, tiled=True)
    stats, sums = attend_near(back, early, keys, values)
    first = attend_far(0, back, live, queries, k_prev, v_prev, stats, sums)
    same, first = lax.optimization_barrier((same, first))
    other = lax.ppermute(same, "c", swap)
    halves = []
    for index in range(2):
        attn = first if index == 0 else attend_far(1, back, live, queries, k_prev, v_prev, stats, sums)
        attn = attn.reshape(GROUP, rows // 2, Q_COLS)
        halves.append(lax.all_to_all(attn, inside, split_axis=0, concat_axis=0, tiled=True))
    at_zero = lax.axis_index("c") == 0
    strip = (groups, 1, 2 * w_o.shape[0], w_o.shape[1])
    even = jnp.where(at_zero, same, other).reshape(strip)
    odd = jnp.where(at_zero, other, same).reshape(strip)
    w_out = jnp.concatenate([even, odd], axis=1).reshape(width, w_o.shape[1])
    return (output(halves, w_out), key_cache, value_cache)


def solution(mesh):
    fine = Mesh(mesh.devices.reshape(-1, 2, 2), ("g", "c", "y"))
    tokens = ("g", "c", "y")
    in_specs = (
        P(tokens, None),
        P(),
        P(tokens, None),
        P(tokens, None),
        P(tokens, None),
        P(),
        P(),
        P(("g", "c")),
    )
    out_specs = (P(tokens, None), P(tokens, None, None), P(tokens, None, None))
    return jax.shard_map(shards, mesh=fine, in_specs=in_specs, out_specs=out_specs, check_vma=False)
```

```python
import functools
import math

import jax
import jax.numpy as jnp
from jax import lax
from jax.experimental import pallas as pl
from jax.experimental.pallas import tpu as pltpu
from jax.sharding import Mesh, PartitionSpec as P

HEADS = 16
KV_HEADS = 8
HEAD_DIM = 128
PAGE = 128
GROUP = 4
CHUNK = 4
THETA = 1000000.0
EPS = 1e-05
NEG = -1e30
VMEM = 56 * 1024 * 1024

Q_COLS = HEADS * HEAD_DIM // GROUP
KV_COLS = KV_HEADS * HEAD_DIM // GROUP
KV_PER = KV_HEADS // GROUP
SHARE = HEADS // KV_HEADS


def normalize(hidden_in, norm_gain):
    values = hidden_in.astype(jnp.float32)
    scale = lax.rsqrt(jnp.mean(values * values, axis=-1, keepdims=True) + EPS)
    return (values * scale * norm_gain[None, :]).astype(jnp.bfloat16)


def page_tables(first_page, pages, prompt_pages, last_fill):
    ends = jnp.cumsum(prompt_pages)
    starts = ends - prompt_pages
    ids = first_page + jnp.arange(pages, dtype=jnp.int32)
    mine = (ids[:, None] >= starts[None, :]) & (ids[:, None] < ends[None, :])
    start = jnp.sum(jnp.where(mine, starts[None, :], 0), axis=1)
    end = jnp.sum(jnp.where(mine, ends[None, :], 0), axis=1)
    fill = jnp.sum(jnp.where(mine, last_fill[None, :], 0), axis=1)
    back = ids - start
    live = jnp.where(ids == end - 1, fill, PAGE)
    return back.astype(jnp.int32), live.astype(jnp.int32)


def rope_tables(back, pages):
    half = HEAD_DIM // 2
    position = (back[:, None] * PAGE + jnp.arange(PAGE, dtype=jnp.int32)[None, :]).reshape(pages * PAGE)
    freq = jnp.power(THETA, -2.0 * jnp.arange(half, dtype=jnp.float32) / HEAD_DIM)
    angle = position.astype(jnp.float32)[:, None] * freq[None, :]
    cosine, sine = jnp.cos(angle), jnp.sin(angle)
    return jnp.concatenate([cosine, cosine], axis=-1), jnp.concatenate([-sine, sine], axis=-1)


def project_body(rotated, spot, x0, x1, x2, x3, w, cosine, sine, *rest):
    outs, held = rest[:-1], rest[-1]
    step = pl.program_id(0)
    for index, x in enumerate((x0, x1, x2, x3)):

        @pl.when(step == index)
        def _(x=x):
            held[...] = x[...]

    tile = 512

    def rows(r, carry):
        at = pl.ds(pl.multiple_of(r * tile, tile), tile)
        product = jnp.dot(held[at, :], w[...], preferred_element_type=jnp.float32)
        c, s = cosine[at, :], sine[at, :]
        column = 0
        for out in outs:
            for head in range(out.shape[1] // HEAD_DIM):
                part = product[:, column : column + HEAD_DIM]
                if column < rotated:
                    part = part * c + pltpu.roll(part, HEAD_DIM // 2, 1) * s
                out[at, head * HEAD_DIM : (head + 1) * HEAD_DIM] = part.astype(jnp.bfloat16)
                column += HEAD_DIM
        return carry

    lax.fori_loop(0, held.shape[0] // tile, rows, 0)


def project(spot, blocks, weights, half, cosine, sine, widths, rotated):
    rows, depth = blocks[0].shape
    columns = sum(widths)
    whole = pl.BlockSpec((rows, depth), lambda s, spot: (0, 0))
    table = pl.BlockSpec((rows, HEAD_DIM), lambda s, spot: (spot[s], 0))
    return pl.pallas_call(
        functools.partial(project_body, rotated),
        grid_spec=pltpu.PrefetchScalarGridSpec(
            num_scalar_prefetch=1,
            grid=(GROUP,),
            in_specs=[whole] * 4
            + [pl.BlockSpec((depth, columns), lambda s, spot: (0, half)), table, table],
            out_specs=[pl.BlockSpec((rows, width), lambda s, spot: (spot[s], 0)) for width in widths],
            scratch_shapes=[pltpu.VMEM((rows, depth), jnp.bfloat16)],
        ),
        out_shape=[jax.ShapeDtypeStruct((GROUP * rows, width), jnp.bfloat16) for width in widths],
        compiler_params=pltpu.CompilerParams(vmem_limit_bytes=VMEM),
        cost_estimate=pl.CostEstimate(
            flops=2 * GROUP * rows * depth * columns, bytes_accessed=GROUP * rows * (depth + columns) * 2, transcendentals=0
        ),
    )(spot, *blocks, weights, cosine, sine)


def scan_chunk(queries, k, v, where, low, state, causal):
    wide = CHUNK * PAGE
    factor = math.log2(math.e) / math.sqrt(HEAD_DIM)
    bias = jnp.where(lax.broadcasted_iota(jnp.int32, (1, wide), 1) >= low, 0.0, NEG)
    fresh = []
    for h in range(KV_PER):
        keys = k[where, h * HEAD_DIM : (h + 1) * HEAD_DIM]
        values = v[where, h * HEAD_DIM : (h + 1) * HEAD_DIM]
        scores = lax.dot_general(
            queries[h], keys, (((1,), (1,)), ((), ())), preferred_element_type=jnp.float32
        ) + bias
        if causal is not None:
            scores = jnp.where(causal, scores, NEG)
        best = jnp.max(scores, axis=1, keepdims=True)
        if state is not None:
            top, total, numer = state[h]
            best = jnp.maximum(top, best)
        expo = jnp.exp2(scores * factor - best * factor)
        part = expo[:, 0:PAGE]
        for piece in range(1, CHUNK):
            part = part + expo[:, piece * PAGE : (piece + 1) * PAGE]
        product = jnp.dot(expo.astype(jnp.bfloat16), values, preferred_element_type=jnp.float32)
        if state is not None:
            shrink = jnp.exp2(top * factor - best * factor)
            part = total * shrink + part
            product = numer * shrink + product
        fresh.append((best, part, product))
    return tuple(fresh)


def query_tiles(q, page):
    at = pl.ds(pl.multiple_of(page * PAGE, PAGE), PAGE)
    return [
        jnp.concatenate(
            [q[at, (h * SHARE + i) * HEAD_DIM : (h * SHARE + i + 1) * HEAD_DIM] for i in range(SHARE)], axis=0
        )
        for h in range(KV_PER)
    ]


def page_at(index, pages):
    per_block = pages // GROUP
    per_half = per_block // 2
    half, rest = lax.div(index, pages // 2), lax.rem(index, pages // 2)
    return lax.div(rest, per_half) * per_block + half * per_half + lax.rem(rest, per_half)


def near_body(back, q, k_own, v_own, stats, sums, k_all, v_all):
    rows = q.shape[0]
    pages = rows // PAGE
    pad = CHUNK * PAGE
    wide = CHUNK * PAGE
    for buffer, own in ((k_all, k_own), (v_all, v_own)):
        buffer[0:pad, :] = jnp.zeros((pad, KV_COLS), jnp.bfloat16)
        buffer[pad:, :] = own[...]
    height = SHARE * PAGE
    row = lax.broadcasted_iota(jnp.int32, (height, wide), 0) % PAGE
    causal = lax.broadcasted_iota(jnp.int32, (height, wide), 1) - (wide - PAGE) <= row
    lower = lax.broadcasted_iota(jnp.int32, (height, HEAD_DIM), 1) < HEAD_DIM // 2

    def page_step(index, carry):
        page = page_at(index, pages)
        reach = jnp.minimum(back[page], page)
        queries = query_tiles(q, page)

        def chunk(i, state, mask):
            first = page + 1 - CHUNK * i
            where = pl.ds(pl.multiple_of(first * PAGE, PAGE), wide)
            low = (CHUNK - 1 + CHUNK * i - reach) * PAGE
            return scan_chunk(queries, k_all, v_all, where, low, state, mask)

        state = chunk(0, None, causal)
        state = lax.fori_loop(1, lax.div(reach, CHUNK) + 1, lambda i, s: chunk(i, s, None), state)
        for h in range(KV_PER):
            best, part, numer = state[h]
            total = jnp.sum(part, axis=1, keepdims=True)
            stats[index, h] = jnp.where(lower, best, total)
            sums[index, h] = numer
        return carry

    lax.fori_loop(0, pages, page_step, 0)


def attend_near(back, q, k_own, v_own):
    rows = q.shape[0]
    smem = pl.BlockSpec(memory_space=pltpu.SMEM)
    vmem = pl.BlockSpec(memory_space=pltpu.VMEM)
    span = rows + CHUNK * PAGE
    state = jax.ShapeDtypeStruct((rows // PAGE, KV_PER, SHARE * PAGE, HEAD_DIM), jnp.float32)
    return pl.pallas_call(
        near_body,
        in_specs=[smem] + [vmem] * 3,
        out_specs=[vmem, vmem],
        out_shape=[state, state],
        scratch_shapes=[pltpu.VMEM((span, KV_COLS), jnp.bfloat16), pltpu.VMEM((span, KV_COLS), jnp.bfloat16)],
        compiler_params=pltpu.CompilerParams(vmem_limit_bytes=VMEM),
        cost_estimate=pl.CostEstimate(flops=12 * 10**9, bytes_accessed=12 * 2**20, transcendentals=10**7),
    )(back, q, k_own, v_own)


def far_body(half, back, live, q, k_prev, v_prev, stats, sums, out):
    rows = q.shape[0]
    pages = rows // PAGE
    wide = CHUNK * PAGE
    height = SHARE * PAGE
    row_in = lax.broadcasted_iota(jnp.int32, (height, 1), 0) % PAGE
    lane = lax.broadcasted_iota(jnp.int32, (height, HEAD_DIM), 1)

    def page_step(index, carry):
        page = page_at(index + half * (pages // 2), pages)
        count = jnp.maximum(back[page] - page, 0)
        queries = query_tiles(q, page)
        state = []
        for h in range(KV_PER):
            pair = stats[index, h]
            best = pair[:, 0:1]
            total = jnp.where(lane == HEAD_DIM // 2, pair, 0.0)
            state.append((best, total, sums[index, h]))

        def chunk(i, state):
            first = pages - CHUNK - CHUNK * i
            where = pl.ds(pl.multiple_of(first * PAGE, PAGE), wide)
            low = (CHUNK + CHUNK * i - count) * PAGE
            return scan_chunk(queries, k_prev, v_prev, where, low, state, None)

        state = lax.fori_loop(0, lax.div(count + CHUNK - 1, CHUNK), chunk, tuple(state))
        alive = row_in < live[page]
        at = pl.ds(pl.multiple_of(index * PAGE, PAGE), PAGE)
        for h in range(KV_PER):
            _, part, numer = state[h]
            total = jnp.sum(part, axis=1, keepdims=True)
            result = jnp.where(alive, numer / total, 0.0).astype(jnp.bfloat16)
            for i in range(SHARE):
                head = h * SHARE + i
                out[at, head * HEAD_DIM : (head + 1) * HEAD_DIM] = result[i * PAGE : (i + 1) * PAGE]
        return carry

    lax.fori_loop(0, pages // 2, page_step, 0)


def attend_far(half, back, live, q, k_prev, v_prev, stats, sums):
    rows = q.shape[0]
    pages = rows // PAGE
    smem = pl.BlockSpec(memory_space=pltpu.SMEM)

    def whole(shape):
        return pl.BlockSpec(shape, lambda n: (0, 0))

    state = pl.BlockSpec((pages // 2,) + stats.shape[1:], lambda n: (half, 0, 0, 0))
    return pl.pallas_call(
        functools.partial(far_body, half),
        grid=(1,),
        in_specs=[smem, smem, whole(q.shape), whole(k_prev.shape), whole(v_prev.shape), state, state],
        out_specs=whole((rows // 2, q.shape[1])),
        out_shape=jax.ShapeDtypeStruct((rows // 2, q.shape[1]), jnp.bfloat16),
        compiler_params=pltpu.CompilerParams(vmem_limit_bytes=VMEM),
        cost_estimate=pl.CostEstimate(flops=4 * 10**9, bytes_accessed=10 * 2**20, transcendentals=4 * 10**6),
    )(back, live, q, k_prev, v_prev, stats, sums)


def pages_body(source, live, k, v, k_out, v_out):
    row = lax.broadcasted_iota(jnp.int32, (PAGE, 1), 0)

    def one(slot, carry):
        page = source[slot]
        at = pl.ds(pl.multiple_of(page * PAGE, PAGE), PAGE)
        keep = row < live[page]
        k_out[slot] = jnp.where(keep, k[at, :].astype(jnp.float32), 0.0).astype(jnp.bfloat16)
        v_out[slot] = jnp.where(keep, v[at, :].astype(jnp.float32), 0.0).astype(jnp.bfloat16)
        return carry

    lax.fori_loop(0, k_out.shape[0], one, 0)


def order_pages(source, live, k, v):
    smem = pl.BlockSpec(memory_space=pltpu.SMEM)
    vmem = pl.BlockSpec(memory_space=pltpu.VMEM)
    shape = jax.ShapeDtypeStruct((k.shape[0] // PAGE, PAGE, k.shape[1]), jnp.bfloat16)
    return pl.pallas_call(
        pages_body,
        in_specs=[smem, smem, vmem, vmem],
        out_specs=[vmem, vmem],
        out_shape=[shape, shape],
        compiler_params=pltpu.CompilerParams(vmem_limit_bytes=VMEM),
        cost_estimate=pl.CostEstimate(flops=10**6, bytes_accessed=4 * 2**20, transcendentals=0),
    )(source, live, k, v)


def output_body(*refs):
    w, out = refs[-2:]
    row = 0
    for a in refs[:-2]:
        rows, depth = a.shape[1:]
        total = jnp.dot(a[0], w[0:depth, :], preferred_element_type=jnp.float32)
        for index in range(1, a.shape[0]):
            total += jnp.dot(a[index], w[index * depth : (index + 1) * depth, :], preferred_element_type=jnp.float32)
        out[row : row + rows, :] = total.astype(jnp.bfloat16)
        row += rows


def output(halves, w):
    parts, rows, depth = halves[0].shape
    columns, tile = w.shape[1], 512
    height = rows * len(halves)
    return pl.pallas_call(
        output_body,
        grid=(columns // tile,),
        in_specs=[pl.BlockSpec((parts, rows, depth), lambda n: (0, 0, 0)) for _ in halves]
        + [pl.BlockSpec((parts * depth, tile), lambda n: (0, n))],
        out_specs=pl.BlockSpec((height, tile), lambda n: (0, n)),
        out_shape=jax.ShapeDtypeStruct((height, columns), jnp.bfloat16),
        compiler_params=pltpu.CompilerParams(vmem_limit_bytes=VMEM),
        cost_estimate=pl.CostEstimate(
            flops=2 * parts * height * depth * columns, bytes_accessed=12 * 2**20, transcendentals=0
        ),
    )(*halves, w)


def shards(hidden_in, norm_gain, w_qk, w_v, w_o, prompt_pages, last_fill, page_slots):
    rows = hidden_in.shape[0]
    inside = ("c", "y")
    place = lax.axis_index("c") * 2 + lax.axis_index("y")
    pages = GROUP * rows // PAGE
    swap = [(0, 1), (1, 0)]

    width = HEADS * HEAD_DIM
    kv_width = KV_HEADS * HEAD_DIM
    depth = w_qk.shape[0]
    split = jnp.concatenate(
        [
            w_qk[:, width:].reshape(depth, GROUP, KV_COLS),
            w_v.reshape(depth, GROUP, KV_COLS),
            w_qk[:, :width].reshape(depth, GROUP, Q_COLS),
        ],
        axis=2,
    ).transpose(1, 0, 2)
    mine = lax.all_to_all(split, inside, split_axis=0, concat_axis=0, tiled=True)
    weights = lax.all_gather(mine.reshape(GROUP * depth, 2 * Q_COLS), "g", axis=0, tiled=True)

    normed = normalize(hidden_in, norm_gain)
    across = lax.ppermute(normed, "y", swap)
    core = lax.ppermute(normed, "c", swap)
    both = lax.ppermute(across, "c", swap)
    spot = jnp.arange(GROUP, dtype=jnp.int32) ^ place

    back, live = page_tables(lax.axis_index("g") * pages, pages, prompt_pages, last_fill)
    cosine, sine = rope_tables(back, pages)

    blocks = (normed, across, core, both)
    keys, values = project(spot, blocks, weights, 0, cosine, sine, (KV_COLS, KV_COLS), KV_COLS)
    groups = lax.axis_size("g")
    onward = [(i, i + 1) for i in range(groups - 1)]
    k_prev = lax.ppermute(keys, "g", onward)
    v_prev = lax.ppermute(values, "g", onward)
    (queries,) = project(spot, blocks, weights, 1, cosine, sine, (Q_COLS,), Q_COLS)

    slots = lax.all_gather(page_slots, "c", axis=0, tiled=False)
    order = jnp.arange(slots.shape[1], dtype=jnp.int32)
    hit = slots[:, None, :] == order[None, :, None]
    source = jnp.sum(jnp.where(hit, order[None, None, :], 0), axis=2)
    source = (source + jnp.arange(2, dtype=jnp.int32)[:, None] * slots.shape[1]).reshape(pages)
    k_pages, v_pages = order_pages(source.astype(jnp.int32), live, keys, values)
    w_out = lax.all_gather(w_o, ("g", "c", "y"), axis=0, tiled=True)
    early, k_pages, v_pages = lax.optimization_barrier((queries, k_pages, v_pages))
    key_cache = lax.all_to_all(k_pages, inside, split_axis=0, concat_axis=2, tiled=True)
    value_cache = lax.all_to_all(v_pages, inside, split_axis=0, concat_axis=2, tiled=True)
    stats, sums = attend_near(back, early, keys, values)
    stats, key_cache, value_cache = lax.optimization_barrier((stats, key_cache, value_cache))
    halves = []
    for index in range(2):
        attn = attend_far(index, back, live, queries, k_prev, v_prev, stats, sums)
        attn = attn.reshape(GROUP, rows // 2, Q_COLS)
        halves.append(lax.all_to_all(attn, inside, split_axis=0, concat_axis=0, tiled=True))
    return (output(halves, w_out), key_cache, value_cache)


def solution(mesh):
    fine = Mesh(mesh.devices.reshape(-1, 2, 2), ("g", "c", "y"))
    tokens = ("g", "c", "y")
    in_specs = (
        P(tokens, None),
        P(),
        P(tokens, None),
        P(tokens, None),
        P(tokens, None),
        P(),
        P(),
        P(("g", "c")),
    )
    out_specs = (P(tokens, None), P(tokens, None, None), P(tokens, None, None))
    return jax.shard_map(shards, mesh=fine, in_specs=in_specs, out_specs=out_specs, check_vma=False)
```
